32 devices in a mesh: rows: 16 (over z, y, x), tm: 2 (over core).
Axes of the slice: x: 2, y: 2, z: 4, core: 2. Of those that a mesh axis runs over, the one named last changes fastest.
Arguments:
- snapshots: bfloat16 [262144, 256], P('rows', 'tm'), may hold values from -6 to 6
- basis: bfloat16 [262144, 32], P(('rows', 'tm')), may hold values from -0.01171875 to 0.01171875
Outputs:
- gram: float32 [560, 560], replicated
- rhs: float32 [560, 32], replicated
The draws below stay inside these ranges and needn't reach their ends.
All inputs are finite; a program needn't handle non-finite values.
Results may differ from the reference program's by a relative error of at most 0.0003.
Values may be sent and summed in bfloat16 or wider, within the bound.
A program may use at most 64 MiB of HBM per device.

```python
import jax
import jax.numpy as jnp
import numpy as np
from jax import lax

R = 32
NROWS = 262144
NT = 256


def spiked(result, own_key, source, target, blocks, factor):
    def block_of(axis_at):
        return (jnp.arange(result.shape[axis_at]) // (result.shape[axis_at] // blocks)).reshape((-1,) + (1,) * (result.ndim - 1 - axis_at))

    first = jax.random.permutation(own_key, blocks)[block_of(target)]
    far = (block_of(target) + blocks // 2) % blocks
    return jnp.where((block_of(source) == first) | (block_of(source) == far), factor * result, result)


def shard_levels(own_key, extent, split, low, high):
    loudness, own = 1.0, jax.random.fold_in(own_key, 6)
    for axis_at, parts in split:
        steps = jnp.exp(jax.random.uniform(jax.random.fold_in(own, axis_at), (parts,), jnp.float32, low / len(split), high / len(split)))
        loudness = loudness * jnp.repeat(steps, extent[axis_at] // parts).reshape([-1 if axis == axis_at else 1 for axis in range(len(extent))])
    return loudness


def normal_values(own_key, extent, scale, limit, split=(), kind=jnp.bfloat16):
    values = jax.random.normal(own_key, extent, jnp.float32) * scale
    if len(split) > 0:
        values = shard_levels(own_key, extent, split, -0.22, 0.18) * values
    return jnp.clip(values, min=-limit, max=limit).astype(kind)


def bell_draw_with(stream_key, dims, spread, reach, pieces, heavy, held_as=jnp.bfloat16):
    entries = spread * jax.random.normal(stream_key, dims, jnp.float32)
    if pieces:
        entries = entries * shard_levels(stream_key, dims, pieces, -0.22, 0.18)
    return jnp.clip(spiked(entries, jax.random.fold_in(stream_key, 3), *heavy), -reach, reach).astype(held_as)


def setup_inputs(seed: int = 0) -> dict:
    keys = jax.random.split(jax.random.key(seed), 3)
    snapshots = bell_draw_with(keys[0], (NROWS, NT), 1.0, 6.0, ((0, 16), (1, 2)), (0, 1, 16, 2.0))
    basis = normal_values(keys[1], (NROWS, R), NROWS ** -0.5, 0.01171875, ((0, 32),))
    return dict(snapshots=snapshots, basis=basis)


def reference(snapshots, basis):
    projected = jnp.dot(basis.T, snapshots, preferred_element_type=jnp.float32)
    series = projected.T
    velocity = jnp.concatenate([series[1:] - series[:-1], jnp.zeros((1, R), jnp.float32)], axis=0)
    weight = (jnp.arange(NT) < NT - 1).astype(jnp.float32)
    upper_pair = np.triu_indices(R)
    quadratic = series[:, upper_pair[0]] * series[:, upper_pair[1]]
    features = jnp.concatenate([series, quadratic], axis=1)
    weighted = features * weight[:, None]
    gram = jnp.dot(weighted.T, features, precision=lax.Precision.HIGHEST) / NT
    rhs = jnp.dot(weighted.T, velocity, precision=lax.Precision.HIGHEST) / NT
    return gram, rhs
```

```python
import functools

import jax
import jax.numpy as jnp
from jax import lax
from jax.experimental import pallas as pl
from jax.experimental.pallas import tpu as pltpu
from jax.sharding import PartitionSpec as P

MESH = pl.DeviceIdType.MESH
CHUNKS = 2


def project_kernel(groups, blocks, owners, snap_hbm, basis_hbm, out_ref, snap, basis, part, landed, gathered,
                   snap_sem, basis_sem, send_basis, recv_basis, send_part, recv_part, send_sum, recv_sum):
    row, block = lax.axis_index("rows"), lax.axis_index("tm")
    world = groups * blocks
    modes, depth = basis_hbm.shape
    share = modes // owners
    piece = depth // CHUNKS

    own_basis = pltpu.make_async_copy(basis_hbm, basis.at[block], basis_sem)
    own_basis.start()
    loads = []
    for i in range(blocks):
        at = lax.rem(block + i, blocks)
        for c in range(CHUNKS):
            span = pl.ds(pl.multiple_of(at * depth + c * piece, 256), piece)
            load = pltpu.make_async_copy(snap_hbm.at[span], snap.at[span], snap_sem.at[i * CHUNKS + c])
            load.start()
            loads.append((load, span))

    barrier = pltpu.get_barrier_semaphore()
    me = row * blocks + block

    def greet(d, carry):
        other = lax.rem(me + d, world)
        pl.semaphore_signal(barrier, inc=1, device_id=(other // blocks, lax.rem(other, blocks)), device_id_type=MESH)
        return carry

    lax.fori_loop(1, world, greet, 0)
    own_basis.wait()
    pl.semaphore_wait(barrier, world - 1)

    sends = []
    for d in range(1, blocks):
        send = pltpu.make_async_remote_copy(
            src_ref=basis.at[block], dst_ref=basis.at[block], send_sem=send_basis.at[d - 1], recv_sem=recv_basis.at[d - 1],
            device_id=(row, lax.rem(block + d, blocks)), device_id_type=MESH)
        send.start()
        sends.append(send)

    total = jnp.zeros((modes, snap.shape[1]), jnp.float32)
    for i in range(blocks):
        at = lax.rem(block + i, blocks)
        if i > 0:
            pltpu.make_async_copy(basis.at[at], basis.at[at], recv_basis.at[blocks - i - 1]).wait()
        for c in range(CHUNKS):
            load, span = loads[i * CHUNKS + c]
            load.wait()
            total += jnp.dot(basis[at, :, c * piece:(c + 1) * piece], snap[span, :], preferred_element_type=jnp.float32)
    for k in range(owners):
        part[k] = total[k * share:(k + 1) * share]

    def scatter(d, carry):
        owner = lax.rem(row + d, owners)

        @pl.when(owner != row)
        def _():
            slot = lax.rem(row - owner + groups, groups) - 1
            pltpu.make_async_remote_copy(
                src_ref=part.at[owner], dst_ref=landed.at[slot], send_sem=send_part, recv_sem=recv_part,
                device_id=(owner, block), device_id_type=MESH).start()

        return carry

    lax.fori_loop(0, owners, scatter, 0)

    def reduce_and_spread():
        pltpu.make_async_copy(landed, landed, recv_part).wait()
        mine = block * owners + row
        gathered[mine] = part[row] + jnp.sum(landed[...], axis=0)

        def spread(d, carry):
            other = lax.rem(me + d, world)
            pltpu.make_async_remote_copy(
                src_ref=gathered.at[mine], dst_ref=gathered.at[mine], send_sem=send_sum, recv_sem=recv_sum,
                device_id=(other // blocks, lax.rem(other, blocks)), device_id_type=MESH).start()
            return carry

        lax.fori_loop(1, world, spread, 0)
        rest = gathered.at[pl.ds(0, owners * blocks - 1)]
        pltpu.make_async_copy(rest, rest, recv_sum).wait()
        for _ in range(groups // owners - 1):
            pltpu.make_async_copy(gathered, gathered, send_sum).wait()
        pltpu.make_async_copy(rest, rest, send_sum).wait()
        sent = part.at[pl.ds(0, owners - 1)]
        pltpu.make_async_copy(sent, sent, send_part).wait()

    if owners == groups:
        reduce_and_spread()
    else:
        pl.when(row < owners)(reduce_and_spread)

        @pl.when(row >= owners)
        def _():
            pltpu.make_async_copy(gathered, gathered, recv_sum).wait()
            pltpu.make_async_copy(part, part, send_part).wait()

    for send in sends:
        send.wait_send()
    steps = snap.shape[1]
    for t in range(blocks):
        for k in range(owners):
            out_ref[k * share:(k + 1) * share, t * steps:(t + 1) * steps] = gathered[t * owners + k]


def gram_kernel(proj_ref, gram_ref, rhs_ref, features, high, low):
    modes, steps = proj_ref.shape
    projected = proj_ref[...]
    velocity = pltpu.roll(projected, steps - 1, 1) - projected
    series = jnp.where(lax.broadcasted_iota(jnp.int32, projected.shape, 1) < steps - 1, projected, 0.0)
    features[0:modes, :] = series
    at = modes
    for i in range(modes):
        features[at:at + modes - i, :] = series[i:i + 1, :] * series[i:, :]
        at += modes - i
    whole = features[...]
    top = whole.astype(jnp.bfloat16)
    high[...] = top
    low[...] = (whole - top.astype(jnp.float32)).astype(jnp.bfloat16)

    def times(a, b):
        return lax.dot_general(a, b, (((1,), (1,)), ((), ())), preferred_element_type=jnp.float32)

    scale = 1.0 / steps
    gram_ref[...] = (times(high[...], high[...]) + times(high[...], low[...]) + times(low[...], high[...])) * scale
    v_high = velocity.astype(jnp.bfloat16)
    v_low = (velocity - v_high.astype(jnp.float32)).astype(jnp.bfloat16)
    rhs_ref[...] = (times(v_high, high[...]) + times(v_high, low[...]) + times(v_low, high[...])) * scale


def shards(groups, blocks, snapshots, basis):
    rows_count, steps = snapshots.shape
    depth, modes = basis.shape
    owners = min(groups, modes // 2)
    share = modes // owners
    vmem = pltpu.CompilerParams(vmem_limit_bytes=40 << 20)
    projected = pl.pallas_call(
        functools.partial(project_kernel, groups, blocks, owners),
        out_shape=jax.ShapeDtypeStruct((modes, steps * blocks), jnp.float32),
        in_specs=[pl.BlockSpec(memory_space=pl.ANY)] * 2,
        out_specs=pl.BlockSpec(memory_space=pltpu.VMEM),
        scratch_shapes=[
            pltpu.VMEM((rows_count, steps), jnp.bfloat16),
            pltpu.VMEM((blocks, modes, depth), jnp.bfloat16),
            pltpu.VMEM((owners, share, steps), jnp.float32),
            pltpu.VMEM((groups - 1, share, steps), jnp.float32),
            pltpu.VMEM((blocks * owners, share, steps), jnp.float32),
            pltpu.SemaphoreType.DMA((blocks * CHUNKS,)),
            pltpu.SemaphoreType.DMA,
            pltpu.SemaphoreType.DMA((blocks - 1,)),
            pltpu.SemaphoreType.DMA((blocks - 1,)),
            pltpu.SemaphoreType.DMA,
            pltpu.SemaphoreType.DMA,
            pltpu.SemaphoreType.DMA,
            pltpu.SemaphoreType.DMA,
        ],
        compiler_params=pltpu.CompilerParams(collective_id=0, has_side_effects=True, vmem_limit_bytes=40 << 20),
    )(snapshots, basis.T)
    count = modes + modes * (modes + 1) // 2
    gram, rhs = pl.pallas_call(
        gram_kernel,
        out_shape=(jax.ShapeDtypeStruct((count, count), jnp.float32), jax.ShapeDtypeStruct((modes, count), jnp.float32)),
        in_specs=[pl.BlockSpec(memory_space=pltpu.VMEM)],
        out_specs=[pl.BlockSpec(memory_space=pltpu.VMEM)] * 2,
        scratch_shapes=[
            pltpu.VMEM((count, steps * blocks), jnp.float32),
            pltpu.VMEM((count, steps * blocks), jnp.bfloat16),
            pltpu.VMEM((count, steps * blocks), jnp.bfloat16),
        ],
        compiler_params=vmem,
    )(projected)
    return gram, rhs.T


def solution(mesh):
    step = functools.partial(shards, mesh.shape["rows"], mesh.shape["tm"])
    return jax.shard_map(step, mesh=mesh, in_specs=(P("rows", "tm"), P(("rows", "tm"), None)), out_specs=(P(), P()), check_vma=False)
```

```python
import functools

import jax
import jax.numpy as jnp
from jax import lax
from jax.experimental import pallas as pl
from jax.experimental.pallas import tpu as pltpu
from jax.sharding import PartitionSpec as P

MESH = pl.DeviceIdType.MESH
CHUNKS = 4


def project_kernel(outer, inner, blocks, snap_hbm, basis_hbm, out_ref, snap, basis, part, landed, crossed, gathered,
                   snap_sem, basis_sem, send_basis, recv_basis, send_sem, recv_sem):
    row, block = lax.axis_index("rows"), lax.axis_index("tm")
    a, b = row // inner, lax.rem(row, inner)
    modes, depth = basis_hbm.shape
    share = modes // inner
    piece = depth // CHUNKS

    own_basis = pltpu.make_async_copy(basis_hbm, basis.at[block], basis_sem)
    own_basis.start()
    loads = []
    for i in range(blocks):
        at = lax.rem(block + i, blocks)
        for c in range(CHUNKS):
            span = pl.ds(pl.multiple_of(at * depth + c * piece, 256), piece)
            load = pltpu.make_async_copy(snap_hbm.at[span], snap.at[span], snap_sem.at[i * CHUNKS + c])
            load.start()
            loads.append((load, span))

    across = [(lax.rem(a + d, outer) * inner + b, block) for d in range(1, outer)]
    within = []
    for e in range(blocks):
        for d in range(inner):
            if d or e:
                within.append((a * inner + lax.rem(b + d, inner), lax.rem(block + e, blocks)))
    barrier = pltpu.get_barrier_semaphore()
    for device in within + across:
        pl.semaphore_signal(barrier, inc=1, device_id=device, device_id_type=MESH)
    own_basis.wait()
    pl.semaphore_wait(barrier, len(within) + len(across))

    sends = []
    for d in range(1, blocks):
        send = pltpu.make_async_remote_copy(
            src_ref=basis.at[block], dst_ref=basis.at[block], send_sem=send_basis.at[d - 1], recv_sem=recv_basis.at[d - 1],
            device_id=(row, lax.rem(block + d, blocks)), device_id_type=MESH)
        send.start()
        sends.append(send)

    total = jnp.zeros((modes, snap.shape[1]), jnp.float32)
    for i in range(blocks):
        at = lax.rem(block + i, blocks)
        if i > 0:
            pltpu.make_async_copy(basis.at[at], basis.at[at], recv_basis.at[blocks - i - 1]).wait()
        for c in range(CHUNKS):
            load, span = loads[i * CHUNKS + c]
            load.wait()
            total += jnp.dot(basis[at, :, c * piece:(c + 1) * piece], snap[span, :], preferred_element_type=jnp.float32)
    for k in range(inner):
        part[k] = total[k * share:(k + 1) * share]

    def send_to(stage, source, target, device):
        pltpu.make_async_remote_copy(
            src_ref=source, dst_ref=target, send_sem=send_sem.at[stage], recv_sem=recv_sem.at[stage],
            device_id=device, device_id_type=MESH).start()

    def wait_all(ref, semaphore):
        pltpu.make_async_copy(ref, ref, semaphore).wait()

    for d in range(1, inner):
        owner = lax.rem(b + d, inner)
        send_to(0, part.at[owner], landed.at[inner - d - 1], (a * inner + owner, block))
    wait_all(landed, recv_sem.at[0])
    crossed[a] = part[b] + jnp.sum(landed[...], axis=0)

    for device in across:
        send_to(1, crossed.at[a], crossed.at[a], device)
    wait_all(crossed.at[pl.ds(0, outer - 1)], recv_sem.at[1])
    mine = block * inner + b
    gathered[mine] = jnp.sum(crossed[...], axis=0)

    for device in within:
        send_to(2, gathered.at[mine], gathered.at[mine], device)
    rest = gathered.at[pl.ds(0, inner * blocks - 1)]
    wait_all(rest, recv_sem.at[2])
    steps = snap.shape[1]
    for t in range(blocks):
        for k in range(inner):
            out_ref[k * share:(k + 1) * share, t * steps:(t + 1) * steps] = gathered[t * inner + k]

    for send in sends:
        send.wait_send()
    wait_all(landed, send_sem.at[0])
    wait_all(crossed.at[pl.ds(0, outer - 1)], send_sem.at[1])
    wait_all(rest, send_sem.at[2])


def gram_kernel(proj_ref, gram_ref, rhs_ref, features, high, low):
    modes, steps = proj_ref.shape
    projected = proj_ref[...]
    velocity = pltpu.roll(projected, steps - 1, 1) - projected
    series = jnp.where(lax.broadcasted_iota(jnp.int32, projected.shape, 1) < steps - 1, projected, 0.0)
    features[0:modes, :] = series
    at = modes
    for i in range(modes):
        features[at:at + modes - i, :] = series[i:i + 1, :] * series[i:, :]
        at += modes - i
    whole = features[...]
    top = whole.astype(jnp.bfloat16)
    high[...] = top
    low[...] = (whole - top.astype(jnp.float32)).astype(jnp.bfloat16)

    def times(a, b):
        return lax.dot_general(a, b, (((1,), (1,)), ((), ())), preferred_element_type=jnp.float32)

    scale = 1.0 / steps
    gram_ref[...] = (times(high[...], high[...]) + times(high[...], low[...]) + times(low[...], high[...])) * scale
    v_high = velocity.astype(jnp.bfloat16)
    v_low = (velocity - v_high.astype(jnp.float32)).astype(jnp.bfloat16)
    rhs_ref[...] = (times(v_high, high[...]) + times(v_high, low[...]) + times(v_low, high[...])) * scale


def shards(groups, blocks, snapshots, basis):
    rows_count, steps = snapshots.shape
    depth, modes = basis.shape
    inner = 1
    while inner * inner < groups:
        inner *= 2
    outer = groups // inner
    share = modes // inner
    vmem = pltpu.CompilerParams(vmem_limit_bytes=40 << 20)
    projected = pl.pallas_call(
        functools.partial(project_kernel, outer, inner, blocks),
        out_shape=jax.ShapeDtypeStruct((modes, steps * blocks), jnp.float32),
        in_specs=[pl.BlockSpec(memory_space=pltpu.HBM)] * 2,
        out_specs=pl.BlockSpec(memory_space=pltpu.VMEM),
        scratch_shapes=[
            pltpu.VMEM((rows_count, steps), jnp.bfloat16),
            pltpu.VMEM((blocks, modes, depth), jnp.bfloat16),
            pltpu.VMEM((inner, share, steps), jnp.float32),
            pltpu.VMEM((inner - 1, share, steps), jnp.float32),
            pltpu.VMEM((outer, share, steps), jnp.float32),
            pltpu.VMEM((blocks * inner, share, steps), jnp.float32),
            pltpu.SemaphoreType.DMA((blocks * CHUNKS,)),
            pltpu.SemaphoreType.DMA,
            pltpu.SemaphoreType.DMA((blocks - 1,)),
            pltpu.SemaphoreType.DMA((blocks - 1,)),
            pltpu.SemaphoreType.DMA((3,)),
            pltpu.SemaphoreType.DMA((3,)),
        ],
        compiler_params=pltpu.CompilerParams(collective_id=0, has_side_effects=True, vmem_limit_bytes=40 << 20),
    )(snapshots, basis.T)
    count = modes + modes * (modes + 1) // 2
    gram, rhs = pl.pallas_call(
        gram_kernel,
        out_shape=(jax.ShapeDtypeStruct((count, count), jnp.float32), jax.ShapeDtypeStruct((modes, count), jnp.float32)),
        in_specs=[pl.BlockSpec(memory_space=pltpu.VMEM)],
        out_specs=[pl.BlockSpec(memory_space=pltpu.VMEM)] * 2,
        scratch_shapes=[
            pltpu.VMEM((count, steps * blocks), jnp.float32),
            pltpu.VMEM((count, steps * blocks), jnp.bfloat16),
            pltpu.VMEM((count, steps * blocks), jnp.bfloat16),
        ],
        compiler_params=vmem,
    )(projected)
    return gram, rhs.T


def solution(mesh):
    step = functools.partial(shards, mesh.shape["rows"], mesh.shape["tm"])
    return jax.shard_map(step, mesh=mesh, in_specs=(P("rows", "tm"), P(("rows", "tm"), None)), out_specs=(P(), P()), check_vma=False)
```

```python
import functools

import jax
import jax.numpy as jnp
from jax import lax
from jax.experimental import pallas as pl
from jax.experimental.pallas import tpu as pltpu
from jax.sharding import PartitionSpec as P

MESH = pl.DeviceIdType.MESH
CHUNKS = 4


def project_kernel(outer, inner, blocks, snap_hbm, basis_hbm, out_ref, snap, basis, part, landed, crossed, gathered,
                   snap_sem, basis_sem, send_basis, recv_basis, send_sem, recv_sem):
    row, block = lax.axis_index("rows"), lax.axis_index("tm")
    a, b = row // inner, lax.rem(row, inner)
    modes, depth = basis_hbm.shape
    share = modes // inner
    piece = depth // CHUNKS

    own_basis = pltpu.make_async_copy(basis_hbm, basis.at[block], basis_sem)
    own_basis.start()
    loads = []
    for i in range(blocks):
        at = lax.rem(block + i, blocks)
        for c in range(CHUNKS):
            span = pl.ds(pl.multiple_of(at * depth + c * piece, 256), piece)
            load = pltpu.make_async_copy(snap_hbm.at[span], snap.at[span], snap_sem.at[i * CHUNKS + c])
            load.start()
            loads.append((load, span))

    across = [(lax.rem(a + d, outer) * inner + b, block) for d in range(1, outer)]
    within = []
    for e in range(blocks):
        for d in range(inner):
            if d or e:
                within.append((a * inner + lax.rem(b + d, inner), lax.rem(block + e, blocks)))
    barrier = pltpu.get_barrier_semaphore()
    for device in within + across:
        pl.semaphore_signal(barrier, inc=1, device_id=device, device_id_type=MESH)
    own_basis.wait()
    pl.semaphore_wait(barrier, len(within) + len(across))

    sends = []
    for d in range(1, blocks):
        send = pltpu.make_async_remote_copy(
            src_ref=basis.at[block], dst_ref=basis.at[block], send_sem=send_basis.at[d - 1], recv_sem=recv_basis.at[d - 1],
            device_id=(row, lax.rem(block + d, blocks)), device_id_type=MESH)
        send.start()
        sends.append(send)

    total = jnp.zeros((modes, snap.shape[1]), jnp.float32)
    for i in range(blocks):
        at = lax.rem(block + i, blocks)
        if i > 0:
            pltpu.make_async_copy(basis.at[at], basis.at[at], recv_basis.at[blocks - i - 1]).wait()
        for c in range(CHUNKS):
            load, span = loads[i * CHUNKS + c]
            load.wait()
            total += jnp.dot(basis[at, :, c * piece:(c + 1) * piece], snap[span, :], preferred_element_type=jnp.float32)
    for k in range(inner):
        part[k] = total[k * share:(k + 1) * share]

    def send_to(stage, source, target, device):
        pltpu.make_async_remote_copy(
            src_ref=source, dst_ref=target, send_sem=send_sem.at[stage], recv_sem=recv_sem.at[stage],
            device_id=device, device_id_type=MESH).start()

    def wait_all(ref, semaphore):
        pltpu.make_async_copy(ref, ref, semaphore).wait()

    for d in range(1, inner):
        owner = lax.rem(b + d, inner)
        send_to(0, part.at[owner], landed.at[inner - d - 1], (a * inner + owner, block))
    wait_all(landed, recv_sem.at[0])
    crossed[a] = part[b] + jnp.sum(landed[...], axis=0)

    for device in across:
        send_to(1, crossed.at[a], crossed.at[a], device)
    wait_all(crossed.at[pl.ds(0, outer - 1)], recv_sem.at[1])
    mine = block * inner + b
    gathered[mine] = jnp.sum(crossed[...], axis=0)

    for device in within:
        send_to(2, gathered.at[mine], gathered.at[mine], device)
    rest = gathered.at[pl.ds(0, inner * blocks - 1)]
    wait_all(rest, recv_sem.at[2])
    steps = snap.shape[1]
    for t in range(blocks):
        for k in range(inner):
            out_ref[k * share:(k + 1) * share, t * steps:(t + 1) * steps] = gathered[t * inner + k]

    for send in sends:
        send.wait_send()
    wait_all(landed, send_sem.at[0])
    wait_all(crossed.at[pl.ds(0, outer - 1)], send_sem.at[1])
    wait_all(rest, send_sem.at[2])


def gram_kernel(proj_ref, gram_ref, rhs_ref, features, high, low):
    modes, steps = proj_ref.shape
    projected = proj_ref[...]
    velocity = pltpu.roll(projected, steps - 1, 1) - projected
    series = jnp.where(lax.broadcasted_iota(jnp.int32, projected.shape, 1) < steps - 1, projected, 0.0)
    features[0:modes, :] = series
    at = modes
    for i in range(modes):
        features[at:at + modes - i, :] = series[i:i + 1, :] * series[i:, :]
        at += modes - i
    whole = features[...]
    top = whole.astype(jnp.bfloat16)
    high[...] = top
    low[...] = (whole - top.astype(jnp.float32)).astype(jnp.bfloat16)

    def times(a, b):
        return lax.dot_general(a, b, (((1,), (1,)), ((), ())), preferred_element_type=jnp.float32)

    scale = 1.0 / steps
    gram_ref[...] = (times(high[...], high[...]) + times(high[...], low[...]) + times(low[...], high[...])) * scale
    v_high = velocity.astype(jnp.bfloat16)
    v_low = (velocity - v_high.astype(jnp.float32)).astype(jnp.bfloat16)
    rhs_ref[...] = (times(v_high, high[...]) + times(v_high, low[...]) + times(v_low, high[...])) * scale


def shards(groups, blocks, snapshots, basis):
    rows_count, steps = snapshots.shape
    depth, modes = basis.shape
    inner = 1
    while inner * inner < groups:
        inner *= 2
    outer = groups // inner
    share = modes // inner
    vmem = pltpu.CompilerParams(vmem_limit_bytes=40 << 20)
    projected = pl.pallas_call(
        functools.partial(project_kernel, outer, inner, blocks),
        out_shape=jax.ShapeDtypeStruct((modes, steps * blocks), jnp.float32),
        in_specs=[pl.BlockSpec(memory_space=pltpu.HBM)] * 2,
        out_specs=pl.BlockSpec(memory_space=pltpu.VMEM),
        scratch_shapes=[
            pltpu.VMEM((rows_count, steps), jnp.bfloat16),
            pltpu.VMEM((blocks, modes, depth), jnp.bfloat16),
            pltpu.VMEM((inner, share, steps), jnp.float32),
            pltpu.VMEM((inner - 1, share, steps), jnp.float32),
            pltpu.VMEM((outer, share, steps), jnp.float32),
            pltpu.VMEM((blocks * inner, share, steps), jnp.float32),
            pltpu.SemaphoreType.DMA((blocks * CHUNKS,)),
            pltpu.SemaphoreType.DMA,
            pltpu.SemaphoreType.DMA((blocks - 1,)),
            pltpu.SemaphoreType.DMA((blocks - 1,)),
            pltpu.SemaphoreType.DMA((3,)),
            pltpu.SemaphoreType.DMA((3,)),
        ],
        compiler_params=pltpu.CompilerParams(collective_id=0, has_side_effects=True, vmem_limit_bytes=40 << 20),
    )(pltpu.with_memory_space_constraint(snapshots, pltpu.HBM), pltpu.with_memory_space_constraint(basis.T, pltpu.HBM))
    count = modes + modes * (modes + 1) // 2
    gram, rhs = pl.pallas_call(
        gram_kernel,
        out_shape=(jax.ShapeDtypeStruct((count, count), jnp.float32), jax.ShapeDtypeStruct((modes, count), jnp.float32)),
        in_specs=[pl.BlockSpec(memory_space=pltpu.VMEM)],
        out_specs=[pl.BlockSpec(memory_space=pltpu.VMEM)] * 2,
        scratch_shapes=[
            pltpu.VMEM((count, steps * blocks), jnp.float32),
            pltpu.VMEM((count, steps * blocks), jnp.bfloat16),
            pltpu.VMEM((count, steps * blocks), jnp.bfloat16),
        ],
        compiler_params=vmem,
    )(projected)
    return gram, rhs.T


def solution(mesh):
    step = functools.partial(shards, mesh.shape["rows"], mesh.shape["tm"])
    return jax.shard_map(step, mesh=mesh, in_specs=(P("rows", "tm"), P(("rows", "tm"), None)), out_specs=(P(), P()), check_vma=False)
```

```python
import functools

import jax
import jax.numpy as jnp
from jax import lax
from jax.experimental import pallas as pl
from jax.experimental.pallas import tpu as pltpu
from jax.sharding import PartitionSpec as P

MESH = pl.DeviceIdType.MESH
CHUNKS = 4


def project_kernel(outer, inner, blocks, snap_hbm, basis_hbm, out_ref, snap, basis, crossed, gathered,
                   snap_sem, basis_sem, send_basis, recv_basis, send_sem, recv_sem):
    row, block = lax.axis_index("rows"), lax.axis_index("tm")
    a, b = row // inner, lax.rem(row, inner)
    modes, depth = basis_hbm.shape
    piece = depth // CHUNKS

    own_basis = pltpu.make_async_copy(basis_hbm, basis.at[block], basis_sem)
    own_basis.start()
    loads = []
    for i in range(blocks):
        at = lax.rem(block + i, blocks)
        for c in range(CHUNKS):
            span = pl.ds(pl.multiple_of(at * depth + c * piece, 256), piece)
            load = pltpu.make_async_copy(snap_hbm.at[span], snap.at[span], snap_sem.at[i * CHUNKS + c])
            load.start()
            loads.append((load, span))

    across = [(lax.rem(a + d, outer) * inner + b, block) for d in range(1, outer)]
    within = []
    for e in range(blocks):
        for d in range(inner):
            if d or e:
                within.append((a * inner + lax.rem(b + d, inner), lax.rem(block + e, blocks)))
    barrier = pltpu.get_barrier_semaphore()
    for device in within + across:
        pl.semaphore_signal(barrier, inc=1, device_id=device, device_id_type=MESH)
    own_basis.wait()
    pl.semaphore_wait(barrier, len(within) + len(across))

    sends = []
    for d in range(1, blocks):
        send = pltpu.make_async_remote_copy(
            src_ref=basis.at[block], dst_ref=basis.at[block], send_sem=send_basis.at[d - 1], recv_sem=recv_basis.at[d - 1],
            device_id=(row, lax.rem(block + d, blocks)), device_id_type=MESH)
        send.start()
        sends.append(send)

    total = jnp.zeros((modes, snap.shape[1]), jnp.float32)
    for i in range(blocks):
        at = lax.rem(block + i, blocks)
        if i > 0:
            pltpu.make_async_copy(basis.at[at], basis.at[at], recv_basis.at[blocks - i - 1]).wait()
        for c in range(CHUNKS):
            load, span = loads[i * CHUNKS + c]
            load.wait()
            total += jnp.dot(basis[at, :, c * piece:(c + 1) * piece], snap[span, :], preferred_element_type=jnp.float32)
    crossed[a] = total

    def send_to(stage, source, target, device):
        pltpu.make_async_remote_copy(
            src_ref=source, dst_ref=target, send_sem=send_sem.at[stage], recv_sem=recv_sem.at[stage],
            device_id=device, device_id_type=MESH).start()

    def wait_all(ref, semaphore):
        pltpu.make_async_copy(ref, ref, semaphore).wait()

    for device in across:
        send_to(0, crossed.at[a], crossed.at[a], device)
    wait_all(crossed.at[pl.ds(0, outer - 1)], recv_sem.at[0])
    mine = block * inner + b
    gathered[mine] = jnp.sum(crossed[...], axis=0)

    for device in within:
        send_to(1, gathered.at[mine], gathered.at[mine], device)
    rest = gathered.at[pl.ds(0, inner * blocks - 1)]
    wait_all(rest, recv_sem.at[1])
    steps = snap.shape[1]
    for t in range(blocks):
        out_ref[:, t * steps:(t + 1) * steps] = jnp.sum(gathered[t * inner:(t + 1) * inner], axis=0)

    for send in sends:
        send.wait_send()
    wait_all(crossed.at[pl.ds(0, outer - 1)], send_sem.at[0])
    wait_all(rest, send_sem.at[1])


def gram_kernel(proj_ref, gram_ref, rhs_ref, features, high, low):
    modes, steps = proj_ref.shape
    projected = proj_ref[...]
    velocity = pltpu.roll(projected, steps - 1, 1) - projected
    series = jnp.where(lax.broadcasted_iota(jnp.int32, projected.shape, 1) < steps - 1, projected, 0.0)
    features[0:modes, :] = series
    at = modes
    for i in range(modes):
        features[at:at + modes - i, :] = series[i:i + 1, :] * series[i:, :]
        at += modes - i
    whole = features[...]
    top = whole.astype(jnp.bfloat16)
    high[...] = top
    low[...] = (whole - top.astype(jnp.float32)).astype(jnp.bfloat16)

    def times(a, b):
        return lax.dot_general(a, b, (((1,), (1,)), ((), ())), preferred_element_type=jnp.float32)

    scale = 1.0 / steps
    gram_ref[...] = (times(high[...], high[...]) + times(high[...], low[...]) + times(low[...], high[...])) * scale
    v_high = velocity.astype(jnp.bfloat16)
    v_low = (velocity - v_high.astype(jnp.float32)).astype(jnp.bfloat16)
    rhs_ref[...] = (times(v_high, high[...]) + times(v_high, low[...]) + times(v_low, high[...])) * scale


def shards(groups, blocks, snapshots, basis):
    rows_count, steps = snapshots.shape
    depth, modes = basis.shape
    inner = 1
    while inner * inner < groups:
        inner *= 2
    outer = groups // inner
    vmem = pltpu.CompilerParams(vmem_limit_bytes=40 << 20)
    projected = pl.pallas_call(
        functools.partial(project_kernel, outer, inner, blocks),
        out_shape=jax.ShapeDtypeStruct((modes, steps * blocks), jnp.float32),
        in_specs=[pl.BlockSpec(memory_space=pltpu.HBM)] * 2,
        out_specs=pl.BlockSpec(memory_space=pltpu.VMEM),
        scratch_shapes=[
            pltpu.VMEM((rows_count, steps), jnp.bfloat16),
            pltpu.VMEM((blocks, modes, depth), jnp.bfloat16),
            pltpu.VMEM((outer, modes, steps), jnp.float32),
            pltpu.VMEM((blocks * inner, modes, steps), jnp.float32),
            pltpu.SemaphoreType.DMA((blocks * CHUNKS,)),
            pltpu.SemaphoreType.DMA,
            pltpu.SemaphoreType.DMA((blocks - 1,)),
            pltpu.SemaphoreType.DMA((blocks - 1,)),
            pltpu.SemaphoreType.DMA((2,)),
            pltpu.SemaphoreType.DMA((2,)),
        ],
        compiler_params=pltpu.CompilerParams(collective_id=0, has_side_effects=True, vmem_limit_bytes=40 << 20),
    )(pltpu.with_memory_space_constraint(snapshots, pltpu.HBM), pltpu.with_memory_space_constraint(basis.T, pltpu.HBM))
    count = modes + modes * (modes + 1) // 2
    gram, rhs = pl.pallas_call(
        gram_kernel,
        out_shape=(jax.ShapeDtypeStruct((count, count), jnp.float32), jax.ShapeDtypeStruct((modes, count), jnp.float32)),
        in_specs=[pl.BlockSpec(memory_space=pltpu.VMEM)],
        out_specs=[pl.BlockSpec(memory_space=pltpu.VMEM)] * 2,
        scratch_shapes=[
            pltpu.VMEM((count, steps * blocks), jnp.float32),
            pltpu.VMEM((count, steps * blocks), jnp.bfloat16),
            pltpu.VMEM((count, steps * blocks), jnp.bfloat16),
        ],
        compiler_params=vmem,
    )(projected)
    return gram, rhs.T


def solution(mesh):
    step = functools.partial(shards, mesh.shape["rows"], mesh.shape["tm"])
    return jax.shard_map(step, mesh=mesh, in_specs=(P("rows", "tm"), P(("rows", "tm"), None)), out_specs=(P(), P()), check_vma=False)
```

```python
import functools

import jax
import jax.numpy as jnp
from jax import lax
from jax.experimental import pallas as pl
from jax.experimental.pallas import tpu as pltpu
from jax.sharding import PartitionSpec as P

MESH = pl.DeviceIdType.MESH
CHUNKS = 2


def project_kernel(outer, inner, blocks, snap_hbm, basis_hbm, out_ref, snap, basis, crossed, gathered,
                   snap_sem, basis_sem, send_basis, recv_basis, send_sem, recv_sem):
    row, block = lax.axis_index("rows"), lax.axis_index("tm")
    a, b = row // inner, lax.rem(row, inner)
    modes, depth = basis_hbm.shape
    piece = depth // CHUNKS

    own_basis = pltpu.make_async_copy(basis_hbm, basis.at[block], basis_sem)
    own_basis.start()
    loads = []
    for i in range(blocks):
        at = lax.rem(block + i, blocks)
        for c in range(CHUNKS):
            span = pl.ds(pl.multiple_of(at * depth + c * piece, 256), piece)
            load = pltpu.make_async_copy(snap_hbm.at[span], snap.at[span], snap_sem.at[i * CHUNKS + c])
            load.start()
            loads.append((load, span))

    across = [(lax.rem(a + d, outer) * inner + b, block) for d in range(1, outer)]
    within = []
    for e in range(blocks):
        for d in range(inner):
            if d or e:
                within.append((a * inner + lax.rem(b + d, inner), lax.rem(block + e, blocks)))
    barrier = pltpu.get_barrier_semaphore()
    for device in within + across:
        pl.semaphore_signal(barrier, inc=1, device_id=device, device_id_type=MESH)
    own_basis.wait()
    pl.semaphore_wait(barrier, len(within) + len(across))

    sends = []
    for d in range(1, blocks):
        send = pltpu.make_async_remote_copy(
            src_ref=basis.at[block], dst_ref=basis.at[block], send_sem=send_basis.at[d - 1], recv_sem=recv_basis.at[d - 1],
            device_id=(row, lax.rem(block + d, blocks)), device_id_type=MESH)
        send.start()
        sends.append(send)

    total = jnp.zeros((modes, snap.shape[1]), jnp.float32)
    for i in range(blocks):
        at = lax.rem(block + i, blocks)
        if i > 0:
            pltpu.make_async_copy(basis.at[at], basis.at[at], recv_basis.at[blocks - i - 1]).wait()
        for c in range(CHUNKS):
            load, span = loads[i * CHUNKS + c]
            load.wait()
            total += jnp.dot(basis[at, :, c * piece:(c + 1) * piece], snap[span, :], preferred_element_type=jnp.float32)
    crossed[a] = total

    def send_to(stage, source, target, device):
        pltpu.make_async_remote_copy(
            src_ref=source, dst_ref=target, send_sem=send_sem.at[stage], recv_sem=recv_sem.at[stage],
            device_id=device, device_id_type=MESH).start()

    def wait_all(ref, semaphore):
        pltpu.make_async_copy(ref, ref, semaphore).wait()

    for device in across:
        send_to(0, crossed.at[a], crossed.at[a], device)
    wait_all(crossed.at[pl.ds(0, outer - 1)], recv_sem.at[0])
    mine = block * inner + b
    gathered[mine] = jnp.sum(crossed[...], axis=0)

    for device in within:
        send_to(1, gathered.at[mine], gathered.at[mine], device)
    rest = gathered.at[pl.ds(0, inner * blocks - 1)]
    wait_all(rest, recv_sem.at[1])
    steps = snap.shape[1]
    for t in range(blocks):
        out_ref[:, t * steps:(t + 1) * steps] = jnp.sum(gathered[t * inner:(t + 1) * inner], axis=0)

    for send in sends:
        send.wait_send()
    wait_all(crossed.at[pl.ds(0, outer - 1)], send_sem.at[0])
    wait_all(rest, send_sem.at[1])


def gram_kernel(proj_ref, gram_ref, rhs_ref, features, high, low):
    modes, steps = proj_ref.shape
    projected = proj_ref[...]
    velocity = pltpu.roll(projected, steps - 1, 1) - projected
    series = jnp.where(lax.broadcasted_iota(jnp.int32, projected.shape, 1) < steps - 1, projected, 0.0)
    features[0:modes, :] = series
    at = modes
    for i in range(modes):
        features[at:at + modes - i, :] = series[i:i + 1, :] * series[i:, :]
        at += modes - i
    whole = features[...]
    top = whole.astype(jnp.bfloat16)
    high[...] = top
    low[...] = (whole - top.astype(jnp.float32)).astype(jnp.bfloat16)

    def times(a, b):
        return lax.dot_general(a, b, (((1,), (1,)), ((), ())), preferred_element_type=jnp.float32)

    scale = 1.0 / steps
    gram_ref[...] = (times(high[...], high[...]) + times(high[...], low[...]) + times(low[...], high[...])) * scale
    v_high = velocity.astype(jnp.bfloat16)
    v_low = (velocity - v_high.astype(jnp.float32)).astype(jnp.bfloat16)
    rhs_ref[...] = (times(v_high, high[...]) + times(v_high, low[...]) + times(v_low, high[...])) * scale


def shards(groups, blocks, snapshots, basis):
    rows_count, steps = snapshots.shape
    depth, modes = basis.shape
    inner = 1
    while inner * inner < groups:
        inner *= 2
    outer = groups // inner
    vmem = pltpu.CompilerParams(vmem_limit_bytes=40 << 20)
    projected = pl.pallas_call(
        functools.partial(project_kernel, outer, inner, blocks),
        out_shape=jax.ShapeDtypeStruct((modes, steps * blocks), jnp.float32),
        in_specs=[pl.BlockSpec(memory_space=pltpu.HBM)] * 2,
        out_specs=pl.BlockSpec(memory_space=pltpu.VMEM),
        scratch_shapes=[
            pltpu.VMEM((rows_count, steps), jnp.bfloat16),
            pltpu.VMEM((blocks, modes, depth), jnp.bfloat16),
            pltpu.VMEM((outer, modes, steps), jnp.float32),
            pltpu.VMEM((blocks * inner, modes, steps), jnp.float32),
            pltpu.SemaphoreType.DMA((blocks * CHUNKS,)),
            pltpu.SemaphoreType.DMA,
            pltpu.SemaphoreType.DMA((blocks - 1,)),
            pltpu.SemaphoreType.DMA((blocks - 1,)),
            pltpu.SemaphoreType.DMA((2,)),
            pltpu.SemaphoreType.DMA((2,)),
        ],
        compiler_params=pltpu.CompilerParams(collective_id=0, has_side_effects=True, vmem_limit_bytes=40 << 20),
    )(pltpu.with_memory_space_constraint(snapshots, pltpu.HBM), pltpu.with_memory_space_constraint(basis.T, pltpu.HBM))
    count = modes + modes * (modes + 1) // 2
    gram, rhs = pl.pallas_call(
        gram_kernel,
        out_shape=(jax.ShapeDtypeStruct((count, count), jnp.float32), jax.ShapeDtypeStruct((modes, count), jnp.float32)),
        in_specs=[pl.BlockSpec(memory_space=pltpu.VMEM)],
        out_specs=[pl.BlockSpec(memory_space=pltpu.VMEM)] * 2,
        scratch_shapes=[
            pltpu.VMEM((count, steps * blocks), jnp.float32),
            pltpu.VMEM((count, steps * blocks), jnp.bfloat16),
            pltpu.VMEM((count, steps * blocks), jnp.bfloat16),
        ],
        compiler_params=vmem,
    )(projected)
    return gram, rhs.T


def solution(mesh):
    step = functools.partial(shards, mesh.shape["rows"], mesh.shape["tm"])
    return jax.shard_map(step, mesh=mesh, in_specs=(P("rows", "tm"), P(("rows", "tm"), None)), out_specs=(P(), P()), check_vma=False)
```

```python
import functools

import jax
import jax.numpy as jnp
from jax import lax
from jax.experimental import pallas as pl
from jax.experimental.pallas import tpu as pltpu
from jax.sharding import PartitionSpec as P

MESH = pl.DeviceIdType.MESH
CHUNKS = 2


def project_kernel(outer, inner, blocks, snap_hbm, basis_hbm, out_ref, snap, basis, crossed, gathered,
                   snap_sem, basis_sem, send_basis, recv_basis, send_sem, recv_sem):
    row, block = lax.axis_index("rows"), lax.axis_index("tm")
    a, b = row // inner, lax.rem(row, inner)
    modes, depth = basis_hbm.shape
    piece = depth // CHUNKS

    own_basis = pltpu.make_async_copy(basis_hbm, basis.at[block], basis_sem)
    own_basis.start()
    loads = []
    for i in range(blocks):
        at = lax.rem(block + i, blocks)
        for c in range(CHUNKS):
            span = pl.ds(pl.multiple_of(at * depth + c * piece, 256), piece)
            load = pltpu.make_async_copy(snap_hbm.at[span], snap.at[span], snap_sem.at[i * CHUNKS + c])
            load.start()
            loads.append((load, span))

    across = [(lax.rem(a + d, outer) * inner + b, block) for d in range(1, outer)]
    within = []
    for e in range(blocks):
        for d in range(inner):
            if d or e:
                within.append((a * inner + lax.rem(b + d, inner), lax.rem(block + e, blocks)))
    barrier = pltpu.get_barrier_semaphore()
    for device in within + across:
        pl.semaphore_signal(barrier, inc=1, device_id=device, device_id_type=MESH)
    own_basis.wait()
    pl.semaphore_wait(barrier, len(within) + len(across))

    sends = []
    for d in range(1, blocks):
        send = pltpu.make_async_remote_copy(
            src_ref=basis.at[block], dst_ref=basis.at[block], send_sem=send_basis.at[d - 1], recv_sem=recv_basis.at[d - 1],
            device_id=(row, lax.rem(block + d, blocks)), device_id_type=MESH)
        send.start()
        sends.append(send)

    total = jnp.zeros((modes, snap.shape[1]), jnp.float32)
    for i in range(blocks):
        at = lax.rem(block + i, blocks)
        if i > 0:
            pltpu.make_async_copy(basis.at[at], basis.at[at], recv_basis.at[blocks - i - 1]).wait()
        for c in range(CHUNKS):
            load, span = loads[i * CHUNKS + c]
            load.wait()
            total += jnp.dot(basis[at, :, c * piece:(c + 1) * piece], snap[span, :], preferred_element_type=jnp.float32)
    crossed[a] = total

    def send_to(stage, source, target, device):
        pltpu.make_async_remote_copy(
            src_ref=source, dst_ref=target, send_sem=send_sem.at[stage], recv_sem=recv_sem.at[stage],
            device_id=device, device_id_type=MESH).start()

    def wait_all(ref, semaphore):
        pltpu.make_async_copy(ref, ref, semaphore).wait()

    for device in across:
        send_to(0, crossed.at[a], crossed.at[a], device)
    wait_all(crossed.at[pl.ds(0, outer - 1)], recv_sem.at[0])
    mine = block * inner + b
    gathered[mine] = jnp.sum(crossed[...], axis=0)

    for device in within:
        send_to(1, gathered.at[mine], gathered.at[mine], device)
    rest = gathered.at[pl.ds(0, inner * blocks - 1)]
    wait_all(rest, recv_sem.at[1])
    steps = snap.shape[1]
    for t in range(blocks):
        out_ref[:, t * steps:(t + 1) * steps] = jnp.sum(gathered[t * inner:(t + 1) * inner], axis=0)

    for send in sends:
        send.wait_send()
    wait_all(crossed.at[pl.ds(0, outer - 1)], send_sem.at[0])
    wait_all(rest, send_sem.at[1])


def gram_kernel(proj_ref, gram_ref, rhs_ref, features, left, right):
    modes, steps = proj_ref.shape
    projected = proj_ref[...]
    velocity = pltpu.roll(projected, steps - 1, 1) - projected
    series = jnp.where(lax.broadcasted_iota(jnp.int32, projected.shape, 1) < steps - 1, projected, 0.0)
    features[0:modes, :] = series
    at = modes
    for i in range(modes):
        features[at:at + modes - i, :] = series[i:i + 1, :] * series[i:, :]
        at += modes - i
    features[at:at + modes, :] = velocity
    whole = features[...]
    high = whole.astype(jnp.bfloat16)
    low = (whole - high.astype(jnp.float32)).astype(jnp.bfloat16)
    left[:, 0:steps] = high
    left[:, steps:2 * steps] = high
    left[:, 2 * steps:3 * steps] = low
    right[:, 0:steps] = high[0:at]
    right[:, steps:2 * steps] = low[0:at]
    right[:, 2 * steps:3 * steps] = high[0:at]
    sums = lax.dot_general(left[...], right[...], (((1,), (1,)), ((), ())), preferred_element_type=jnp.float32) * (1.0 / steps)
    gram_ref[...] = sums[0:at]
    rhs_ref[...] = sums[at:]


def shards(groups, blocks, snapshots, basis):
    rows_count, steps = snapshots.shape
    depth, modes = basis.shape
    inner = 1
    while inner * inner < groups:
        inner *= 2
    outer = groups // inner
    vmem = pltpu.CompilerParams(vmem_limit_bytes=40 << 20)
    projected = pl.pallas_call(
        functools.partial(project_kernel, outer, inner, blocks),
        out_shape=jax.ShapeDtypeStruct((modes, steps * blocks), jnp.float32),
        in_specs=[pl.BlockSpec(memory_space=pltpu.HBM)] * 2,
        out_specs=pl.BlockSpec(memory_space=pltpu.VMEM),
        scratch_shapes=[
            pltpu.VMEM((rows_count, steps), jnp.bfloat16),
            pltpu.VMEM((blocks, modes, depth), jnp.bfloat16),
            pltpu.VMEM((outer, modes, steps), jnp.float32),
            pltpu.VMEM((blocks * inner, modes, steps), jnp.float32),
            pltpu.SemaphoreType.DMA((blocks * CHUNKS,)),
            pltpu.SemaphoreType.DMA,
            pltpu.SemaphoreType.DMA((blocks - 1,)),
            pltpu.SemaphoreType.DMA((blocks - 1,)),
            pltpu.SemaphoreType.DMA((2,)),
            pltpu.SemaphoreType.DMA((2,)),
        ],
        compiler_params=pltpu.CompilerParams(collective_id=0, has_side_effects=True, vmem_limit_bytes=40 << 20),
    )(pltpu.with_memory_space_constraint(snapshots, pltpu.HBM), pltpu.with_memory_space_constraint(basis.T, pltpu.HBM))
    count = modes + modes * (modes + 1) // 2
    gram, rhs = pl.pallas_call(
        gram_kernel,
        out_shape=(jax.ShapeDtypeStruct((count, count), jnp.float32), jax.ShapeDtypeStruct((modes, count), jnp.float32)),
        in_specs=[pl.BlockSpec(memory_space=pltpu.VMEM)],
        out_specs=[pl.BlockSpec(memory_space=pltpu.VMEM)] * 2,
        scratch_shapes=[
            pltpu.VMEM((count + modes, steps * blocks), jnp.float32),
            pltpu.VMEM((count + modes, 3 * steps * blocks), jnp.bfloat16),
            pltpu.VMEM((count, 3 * steps * blocks), jnp.bfloat16),
        ],
        compiler_params=vmem,
    )(projected)
    return gram, rhs.T


def solution(mesh):
    step = functools.partial(shards, mesh.shape["rows"], mesh.shape["tm"])
    return jax.shard_map(step, mesh=mesh, in_specs=(P("rows", "tm"), P(("rows", "tm"), None)), out_specs=(P(), P()), check_vma=False)
```

```python
import functools

import jax
import jax.numpy as jnp
from jax import lax
from jax.experimental import pallas as pl
from jax.experimental.pallas import tpu as pltpu
from jax.sharding import PartitionSpec as P

MESH = pl.DeviceIdType.MESH
CHUNKS = 2


def project_kernel(outer, inner, blocks, snap_hbm, basis_hbm, out_ref, snap, basis, crossed, gathered,
                   snap_sem, basis_sem, send_basis, recv_basis, send_sem, recv_sem):
    row, block = lax.axis_index("rows"), lax.axis_index("tm")
    a, b = row // inner, lax.rem(row, inner)
    modes, depth = basis_hbm.shape
    piece = depth // CHUNKS

    own_basis = pltpu.make_async_copy(basis_hbm, basis.at[block], basis_sem)
    own_basis.start()
    loads = []
    for i in range(blocks):
        at = lax.rem(block + i, blocks)
        for c in range(CHUNKS):
            span = pl.ds(pl.multiple_of(at * depth + c * piece, 256), piece)
            load = pltpu.make_async_copy(snap_hbm.at[span], snap.at[span], snap_sem.at[i * CHUNKS + c])
            load.start()
            loads.append((load, span))

    across = [(lax.rem(a + d, outer) * inner + b, block) for d in range(1, outer)]
    within = []
    for d in range(inner - 1, -1, -1):
        for e in range(blocks):
            if d or e:
                within.append((a * inner + lax.rem(b + d, inner), lax.rem(block + e, blocks)))
    barrier = pltpu.get_barrier_semaphore()
    for device in within + across:
        pl.semaphore_signal(barrier, inc=1, device_id=device, device_id_type=MESH)
    own_basis.wait()
    pl.semaphore_wait(barrier, len(within) + len(across))

    sends = []
    for d in range(1, blocks):
        send = pltpu.make_async_remote_copy(
            src_ref=basis.at[block], dst_ref=basis.at[block], send_sem=send_basis.at[d - 1], recv_sem=recv_basis.at[d - 1],
            device_id=(row, lax.rem(block + d, blocks)), device_id_type=MESH)
        send.start()
        sends.append(send)

    total = jnp.zeros((modes, snap.shape[1]), jnp.float32)
    for i in range(blocks):
        at = lax.rem(block + i, blocks)
        if i > 0:
            pltpu.make_async_copy(basis.at[at], basis.at[at], recv_basis.at[blocks - i - 1]).wait()
        for c in range(CHUNKS):
            load, span = loads[i * CHUNKS + c]
            load.wait()
            total += jnp.dot(basis[at, :, c * piece:(c + 1) * piece], snap[span, :], preferred_element_type=jnp.float32)
    crossed[a] = total

    def send_to(stage, source, target, device):
        pltpu.make_async_remote_copy(
            src_ref=source, dst_ref=target, send_sem=send_sem.at[stage], recv_sem=recv_sem.at[stage],
            device_id=device, device_id_type=MESH).start()

    def wait_all(ref, semaphore):
        pltpu.make_async_copy(ref, ref, semaphore).wait()

    for device in across:
        send_to(0, crossed.at[a], crossed.at[a], device)
    wait_all(crossed.at[pl.ds(0, outer - 1)], recv_sem.at[0])
    mine = block * inner + b
    gathered[mine] = jnp.sum(crossed[...], axis=0)

    for device in within:
        send_to(1, gathered.at[mine], gathered.at[mine], device)
    rest = gathered.at[pl.ds(0, inner * blocks - 1)]
    wait_all(rest, recv_sem.at[1])
    steps = snap.shape[1]
    for t in range(blocks):
        out_ref[:, t * steps:(t + 1) * steps] = jnp.sum(gathered[t * inner:(t + 1) * inner], axis=0)

    for send in sends:
        send.wait_send()
    wait_all(crossed.at[pl.ds(0, outer - 1)], send_sem.at[0])
    wait_all(rest, send_sem.at[1])


def gram_kernel(proj_ref, gram_ref, rhs_ref, features, left, right):
    modes, steps = proj_ref.shape
    projected = proj_ref[...]
    velocity = pltpu.roll(projected, steps - 1, 1) - projected
    series = jnp.where(lax.broadcasted_iota(jnp.int32, projected.shape, 1) < steps - 1, projected, 0.0)
    features[0:modes, :] = series
    at = modes
    for i in range(modes):
        features[at:at + modes - i, :] = series[i:i + 1, :] * series[i:, :]
        at += modes - i
    features[at:at + modes, :] = velocity
    whole = features[...]
    high = whole.astype(jnp.bfloat16)
    low = (whole - high.astype(jnp.float32)).astype(jnp.bfloat16)
    left[:, 0:steps] = high
    left[:, steps:2 * steps] = high
    left[:, 2 * steps:3 * steps] = low
    right[:, 0:steps] = high[0:at]
    right[:, steps:2 * steps] = low[0:at]
    right[:, 2 * steps:3 * steps] = high[0:at]
    sums = lax.dot_general(left[...], right[...], (((1,), (1,)), ((), ())), preferred_element_type=jnp.float32) * (1.0 / steps)
    gram_ref[...] = sums[0:at]
    rhs_ref[...] = sums[at:]


def shards(groups, blocks, snapshots, basis):
    rows_count, steps = snapshots.shape
    depth, modes = basis.shape
    inner = 1
    while inner * inner < groups:
        inner *= 2
    outer = groups // inner
    vmem = pltpu.CompilerParams(vmem_limit_bytes=40 << 20)
    projected = pl.pallas_call(
        functools.partial(project_kernel, outer, inner, blocks),
        out_shape=jax.ShapeDtypeStruct((modes, steps * blocks), jnp.float32),
        in_specs=[pl.BlockSpec(memory_space=pltpu.HBM)] * 2,
        out_specs=pl.BlockSpec(memory_space=pltpu.VMEM),
        scratch_shapes=[
            pltpu.VMEM((rows_count, steps), jnp.bfloat16),
            pltpu.VMEM((blocks, modes, depth), jnp.bfloat16),
            pltpu.VMEM((outer, modes, steps), jnp.float32),
            pltpu.VMEM((blocks * inner, modes, steps), jnp.float32),
            pltpu.SemaphoreType.DMA((blocks * CHUNKS,)),
            pltpu.SemaphoreType.DMA,
            pltpu.SemaphoreType.DMA((blocks - 1,)),
            pltpu.SemaphoreType.DMA((blocks - 1,)),
            pltpu.SemaphoreType.DMA((2,)),
            pltpu.SemaphoreType.DMA((2,)),
        ],
        compiler_params=pltpu.CompilerParams(collective_id=0, has_side_effects=True, vmem_limit_bytes=40 << 20),
    )(pltpu.with_memory_space_constraint(snapshots, pltpu.HBM), pltpu.with_memory_space_constraint(basis.T, pltpu.HBM))
    count = modes + modes * (modes + 1) // 2
    gram, rhs = pl.pallas_call(
        gram_kernel,
        out_shape=(jax.ShapeDtypeStruct((count, count), jnp.float32), jax.ShapeDtypeStruct((modes, count), jnp.float32)),
        in_specs=[pl.BlockSpec(memory_space=pltpu.VMEM)],
        out_specs=[pl.BlockSpec(memory_space=pltpu.VMEM)] * 2,
        scratch_shapes=[
            pltpu.VMEM((count + modes, steps * blocks), jnp.float32),
            pltpu.VMEM((count + modes, 3 * steps * blocks), jnp.bfloat16),
            pltpu.VMEM((count, 3 * steps * blocks), jnp.bfloat16),
        ],
        compiler_params=vmem,
    )(projected)
    return gram, rhs.T


def solution(mesh):
    step = functools.partial(shards, mesh.shape["rows"], mesh.shape["tm"])
    return jax.shard_map(step, mesh=mesh, in_specs=(P("rows", "tm"), P(("rows", "tm"), None)), out_specs=(P(), P()), check_vma=False)
```
